128 devices in a mesh: grp: 2 (over y_lo), dev: 64 (over z, x, y_hi, core).
Axes of the slice: x: 4, y: 4 (y_hi: 2, y_lo: 2; y = y_hi * 2 + y_lo), z: 4, core: 2. Of those that a mesh axis runs over, the one named last changes fastest.
Arguments:
- images: bfloat16 [114688, 1152], P(('grp', 'dev')), may hold values from -6 to 6
- texts: bfloat16 [114688, 1152], P(('grp', 'dev')), may hold values from -6 to 6
- image_partner: int32 [114688], P(('grp', 'dev')), may hold values from 0 to 114687, as said below
- text_partner: int32 [114688], P(('grp', 'dev')), may hold values from 0 to 114687, as said below
Outputs:
- grad_images: float32 [114688, 1152], P(('grp', 'dev'))
- grad_texts: float32 [114688, 1152], P(('grp', 'dev'))
The draws below stay inside these ranges and needn't reach their ends.
Inputs may be any that keep to these rules, and one draw needn't show every extreme that they name: image_partner is a permutation of the text indices that maps each block of 896 rows onto itself. text_partner is the inverse permutation of image_partner: text_partner[image_partner[i]] == i.
All inputs are finite; a program needn't handle non-finite values.
Results may differ from the reference program's by a relative error of at most 0.0017.
Values may be sent and summed in bfloat16 or wider, within the bound.
No kernel may reach another device: no remote copies, remote signals or barrier semaphores. Data moves between devices by JAX's collectives and lax.ppermute only.
A program may use at most 128 MiB of HBM per device.

```python
import math
import jax
import jax.numpy as jnp
from jax import lax

D = 1152
B_DEV = 896
ROUNDS = 2
BATCH = 114688


def block_permutation(key):
    count = BATCH // B_DEV
    keys = jax.random.split(key, count)
    perms = jax.vmap(lambda single: jax.random.permutation(single, B_DEV))(keys)
    starts = jnp.arange(count, dtype=jnp.int32) * B_DEV
    return (perms.astype(jnp.int32) + starts[:, None]).reshape(BATCH).astype(jnp.int32)


def draw_image_partner(key, part):
    matched = block_permutation(key)
    return matched


def draw_text_partner(key, part):
    matched = block_permutation(key)
    return jnp.argsort(matched, stable=True).astype(jnp.int32)


def steps_of(key, dims, shards, smallest, largest):
    level, own = 1.0, jax.random.fold_in(key, 6)
    for axis_at, blocks in shards:
        heights = jnp.exp(jax.random.uniform(jax.random.fold_in(own, axis_at), (blocks,), jnp.float32, smallest / len(shards), largest / len(shards)))
        level = level * jnp.repeat(heights, dims[axis_at] // blocks).reshape([-1 if axis == axis_at else 1 for axis in range(len(dims))])
    return level


def scatter_about(own_key, extent, width, bound, cuts=(), kind=jnp.bfloat16):
    values = width * jax.random.normal(own_key, extent, jnp.float32)
    if cuts:
        values = values * steps_of(own_key, extent, cuts, -0.22, 0.18)
    return jnp.clip(values, -bound, bound).astype(kind)


def setup_inputs(seed: int = 0) -> dict:
    key_of = jax.random.split(jax.random.key(seed), 5)
    images = scatter_about(key_of[0], (BATCH, D), 1.0, 6.0, ((0, 128),))
    texts = scatter_about(key_of[1], (BATCH, D), 1.0, 6.0, ((0, 128),))
    image_partner = draw_image_partner(jax.random.fold_in(key_of[4], 71), 0)
    text_partner = draw_text_partner(jax.random.fold_in(key_of[4], 71), 0)
    return {"images": images, "texts": texts, "image_partner": image_partner, "text_partner": text_partner}


def weights_of(logits, signs, temp):
    return (-signs * jax.nn.sigmoid(-signs * logits) * temp).astype(jnp.bfloat16)

def reference(images, texts, image_partner, text_partner):
    temp = 2.0 / math.sqrt(D)
    count = BATCH // B_DEV
    image_blocks = images.reshape(count, B_DEV, D)
    text_blocks = texts.reshape(count, B_DEV, D)
    ip_blocks = image_partner.reshape(count, B_DEV)
    tp_blocks = text_partner.reshape(count, B_DEV)
    row_blocks = jnp.arange(BATCH, dtype=jnp.int32).reshape(count, B_DEV)

    def tile_grads(items):
        a_img, a_ip, a_rows, b_txt, b_tp, b_rows = items
        logits = temp * jnp.dot(a_img, b_txt.T, preferred_element_type=jnp.float32) - 2.0
        sign_img = jnp.where(a_ip[:, None] == b_rows[None, :], 1.0, -1.0).astype(jnp.float32)
        sign_txt = jnp.where(b_tp[None, :] == a_rows[:, None], 1.0, -1.0).astype(jnp.float32)
        weight_img = weights_of(logits, sign_img, temp)
        weight_txt = weights_of(logits, sign_txt, temp)
        grad_img = jnp.dot(weight_img, b_txt, preferred_element_type=jnp.float32)
        grad_txt = jnp.dot(weight_txt.T, a_img, preferred_element_type=jnp.float32)
        return (grad_img, grad_txt)
    offsets = [0] + list(range(1, ROUNDS + 1)) + [-r for r in range(1, ROUNDS + 1)]
    grad_img = jnp.zeros((count, B_DEV, D), jnp.float32)
    grad_txt = jnp.zeros((count, B_DEV, D), jnp.float32)
    for offset in offsets:
        moved_txt = jnp.roll(text_blocks, -offset, axis=0)
        moved_tp = jnp.roll(tp_blocks, -offset, axis=0)
        moved_rows = jnp.roll(row_blocks, -offset, axis=0)
        part_img, part_txt = lax.map(tile_grads, (image_blocks, ip_blocks, row_blocks, moved_txt, moved_tp, moved_rows))
        grad_img = grad_img + part_img
        grad_txt = grad_txt + jnp.roll(part_txt, offset, axis=0)
    return (grad_img.reshape(BATCH, D), grad_txt.reshape(BATCH, D))
```

```python
import functools

import jax
import jax.numpy as jnp
from jax import lax
from jax.experimental import pallas as pl
from jax.experimental.pallas import tpu as pltpu
from jax.sharding import PartitionSpec as P

AXES = ("grp", "dev")
LOG2E = 1.4426950408889634
NT = (((1,), (1,)), ((), ()))
PIECES = (256, 256, 192, 128, 64)
DEVICES = range(128)


def place(device):
    return (device >> 6, (device >> 4) & 3, (device >> 2) & 3, (device >> 1) & 1, device & 1)


def device_at(grp, z, x, half, core):
    return (grp << 6) | ((z & 3) << 4) | ((x & 3) << 2) | (half << 1) | core


def at_y(y, z, x, core):
    return device_at(y & 1, z, x, (y & 3) >> 1, core)


CORE_SWAP = [(d, d ^ 1) for d in DEVICES]
HALF_SWAP = [(d, d ^ 2) for d in DEVICES]


def along_x(device):
    grp, z, x, half, core = place(device)
    return device_at(grp, z, x + (1 if half == 0 else -1), half, core)


ALONG_X = [(d, along_x(d)) for d in DEVICES]


def along_z():
    route = []
    for grp in (0, 1):
        for core in (0, 1):
            for z in range(3):
                route.append((device_at(grp, z, 0, 0, core), device_at(grp, z + 1, 0, 0, core)))
                route.append((device_at(grp, z + 1, 3, 1, core), device_at(grp, z, 3, 1, core)))
    return route


ALONG_Z = along_z()

SEAM = ((2, 3, 1, 0), (1, 0, 2, 3), (3, 3, 0, 0), (0, 0, 3, 3))


def pairs(build):
    route = []
    for y_from, at_from, y_to, at_to in SEAM:
        for core in (0, 1):
            route += build(y_from, at_from, y_to, at_to, core)
    return route


def across_seam(stacked, is_source, in_source_plane):
    quarter = stacked.shape[0] // 4
    sixteenth = quarter // 4
    spread = 0
    for k in (1, 2, 3):
        route = pairs(lambda y, a, v, b, c: [(at_y(y, a, a, c), at_y(y, a, a + k, c))])
        spread = spread + lax.ppermute(stacked[k * quarter : (k + 1) * quarter], AXES, route)
    spread = jnp.where(is_source, stacked[:quarter], spread)
    lanes = 0
    for k in (1, 2, 3):
        route = pairs(lambda y, a, v, b, c: [(at_y(y, a, x, c), at_y(y, a + k, x, c)) for x in range(4)])
        lanes = lanes + lax.ppermute(spread[k * sixteenth : (k + 1) * sixteenth], AXES, route)
    lanes = jnp.where(in_source_plane, spread[:sixteenth], lanes)
    route = pairs(lambda y, a, v, b, c: [(at_y(y, z, x, c), at_y(v, z, x, c)) for z in range(4) for x in range(4)])
    lanes = lax.ppermute(lanes, AXES, route)
    rows = []
    for k in range(4):
        route = pairs(lambda y, a, v, b, c: [(at_y(v, a + k, x, c), at_y(v, b, x, c)) for x in range(4)])
        rows.append(lax.ppermute(lanes, AXES, route))
    rows = jnp.concatenate(rows, axis=0)
    whole = []
    for k in range(4):
        route = pairs(lambda y, a, v, b, c: [(at_y(v, b, a + k, c), at_y(v, b, b, c))])
        whole.append(lax.ppermute(rows, AXES, route))
    return jnp.concatenate(whole, axis=0)


def weights(product, temp, positive):
    exponent = product * (-temp * LOG2E) + 2.0 * LOG2E
    if positive is None:
        return (temp / (1.0 + jnp.exp2(exponent))).astype(jnp.bfloat16)
    exponent = jnp.where(positive, -exponent, exponent)
    return (jnp.where(positive, -temp, temp) / (1.0 + jnp.exp2(exponent))).astype(jnp.bfloat16)


def block_body(count, own, temp, *refs):
    rows, others, rest = refs[0], refs[1 : 1 + count], refs[1 + count :]
    if own:
        partner, out, stacked, weight = rest
    else:
        total, out, stacked, weight = rest

    @pl.when(pl.program_id(0) == 0)
    def _():
        at = 0
        for other in others:
            stacked[at : at + other.shape[0], :] = other[...]
            at += other.shape[0]

    left = rows[...]
    many = stacked.shape[0]
    for at in range(0, many, 256):
        end = min(many, at + 256)
        product = lax.dot_general(left, stacked[at:end, :], NT, preferred_element_type=jnp.float32)
        positive = None
        if own and at < others[0].shape[0]:
            column = at + lax.broadcasted_iota(jnp.int32, product.shape, 1)
            positive = column == partner[...]
        weight[:, at:end] = weights(product, temp, positive)
    grads = jnp.dot(weight[...], stacked[...], preferred_element_type=jnp.float32)
    out[...] = grads if own else grads + total[...]


def accumulate(rows, others, halves, size, temp, partner=None, total=None, block=448):
    height, width = rows.shape
    count = len(others)
    many = count * size
    own = partner is not None
    by_row = lambda i: (i, 0)
    last = partner if own else total
    in_specs = [pl.BlockSpec((block, width), by_row)]
    in_specs += [pl.BlockSpec((size, width), lambda i, half=half: (half, 0)) for half in halves]
    in_specs += [pl.BlockSpec((block, last.shape[1]), by_row)]
    return pl.pallas_call(
        functools.partial(block_body, count, own, temp),
        grid=(height // block,),
        in_specs=in_specs,
        out_specs=pl.BlockSpec((block, width), by_row),
        out_shape=jax.ShapeDtypeStruct((height, width), jnp.float32),
        scratch_shapes=[
            pltpu.VMEM((many, width), jnp.bfloat16),
            pltpu.VMEM((block, many), jnp.bfloat16),
        ],
        input_output_aliases={} if own else {count + 1: 0},
        compiler_params=pltpu.CompilerParams(vmem_limit_bytes=48 * 2**20),
        cost_estimate=pl.CostEstimate(
            flops=4 * height * many * width,
            bytes_accessed=height * width * (6 if own else 10) + many * width * 2,
            transcendentals=2 * height * many,
        ),
    )(rows, *others, last)


def shards(images, texts, image_partner, text_partner):
    height, width = images.shape
    temp = 2.0 * width ** (-0.5)
    index = lax.axis_index(AXES)
    core, half, x, z, grp = index & 1, (index >> 1) & 1, (index >> 2) & 3, (index >> 4) & 3, index >> 6
    first_passes_on = core == half
    carried = ((half == 0) & (x == 0)) | ((half == 1) & (x == 3))
    source_z = jnp.where(half == 0, 0, 3)
    in_source_plane = z == source_z
    is_source = in_source_plane & (x == source_z)

    pieces = []
    at = 0
    for size in PIECES:
        pieces.append(jnp.concatenate([texts[at : at + size], images[at : at + size]], axis=0))
        at += size

    swapped = []
    for j, piece in enumerate(pieces):
        if j >= 2:
            piece, swapped[j - 2] = lax.optimization_barrier((piece, swapped[j - 2]))
        swapped.append(lax.ppermute(piece, AXES, HALF_SWAP))
    partner_images = lax.ppermute(images, AXES, CORE_SWAP)
    partner_texts = lax.ppermute(texts, AXES, CORE_SWAP)

    seam = across_seam(jnp.concatenate(pieces, axis=0), is_source, in_source_plane)

    start = index * height
    grad_images = accumulate(
        images, (texts, partner_texts), (0, 0), height, temp, partner=(image_partner - start)[:, None]
    )
    grad_texts = accumulate(
        texts, (images, partner_images), (0, 0), height, temp, partner=(text_partner - start)[:, None]
    )
    at = 0
    for size, one in zip(PIECES, swapped):
        two = lax.ppermute(one, AXES, ALONG_X)
        two_z = lax.ppermute(two, AXES, ALONG_Z)
        two = jnp.where(carried, two_z + seam[at : at + 2 * size], two)
        at += 2 * size
        three = lax.ppermute(jnp.where(first_passes_on, one, two), AXES, CORE_SWAP)
        others = (one, two, three)
        grad_images = accumulate(images, others, (0, 0, 0), size, temp, total=grad_images)
        grad_texts = accumulate(texts, others, (1, 1, 1), size, temp, total=grad_texts)
    return (grad_images, grad_texts)


def solution(mesh):
    return jax.shard_map(
        shards,
        mesh=mesh,
        in_specs=(P(AXES, None), P(AXES, None), P(AXES), P(AXES)),
        out_specs=(P(AXES, None), P(AXES, None)),
        check_vma=False,
    )
```

```python
import functools

import jax
import jax.numpy as jnp
from jax import lax
from jax.experimental import pallas as pl
from jax.experimental.pallas import tpu as pltpu
from jax.sharding import PartitionSpec as P

AXES = ("grp", "dev")
LOG2E = 1.4426950408889634
NT = (((1,), (1,)), ((), ()))
BLOCK = 448
STEP = 256
PIECES = (256, 256, 224, 160)
DEVICES = range(128)
NO_COVER = pl.CostEstimate(flops=1, bytes_accessed=1, transcendentals=0)


CORE_SWAP = [(d, d ^ 1) for d in DEVICES]
HALF_SWAP = [(d, d ^ 2) for d in DEVICES]
HAND_ON = [(d, (d + 4 if d & 2 == 0 else d - 4) % 128) for d in DEVICES]
HAND_ON_WITHIN = [(d, to) for d, to in HAND_ON if (d >> 6) == (to >> 6)]
AHEAD = [(d, (d - 2) % 128) for d in DEVICES]
BEHIND = [(d, (d + 2) % 128) for d in DEVICES]


ACROSS = [(62, 64), (63, 65), (64, 62), (65, 63), (126, 0), (127, 1), (0, 126), (1, 127)]


def weights(product, temp, positive):
    exponent = product * (-temp * LOG2E) + 2.0 * LOG2E
    if positive is None:
        return (temp / (1.0 + jnp.exp2(exponent))).astype(jnp.bfloat16)
    exponent = jnp.where(positive, -exponent, exponent)
    return (jnp.where(positive, -temp, temp) / (1.0 + jnp.exp2(exponent))).astype(jnp.bfloat16)


def gradient(left, stack, weight, temp, partner):
    many = stack.shape[0]
    for at in range(0, many, STEP):
        end = min(many, at + STEP)
        product = lax.dot_general(left, stack[at:end, :], NT, preferred_element_type=jnp.float32)
        positive = None
        if partner is not None and at < many // 2:
            positive = partner == at + lax.broadcasted_iota(jnp.int32, product.shape, 1)
        weight[:, at:end] = weights(product, temp, positive)
    return jnp.dot(weight[...], stack[...], preferred_element_type=jnp.float32)


def own_body(temp, waits, rows, own, other, partner, *refs):
    total, kept, token, stack, weight, sems = refs[waits:]
    token[...] = jnp.zeros_like(token)
    height = kept.shape[0]
    copies = [
        pltpu.make_async_copy(rows, kept, sems.at[0]),
        pltpu.make_async_copy(own, stack.at[pl.ds(0, height)], sems.at[1]),
        pltpu.make_async_copy(other, stack.at[pl.ds(height, height)], sems.at[2]),
    ]
    for copy in copies:
        copy.start()
    for copy in copies:
        copy.wait()
    for b in range(height // BLOCK):
        here = slice(b * BLOCK, (b + 1) * BLOCK)
        total[here, :] = gradient(kept[here, :], stack, weight.at[b % 2], temp, partner[here, :])


TOKEN = jax.ShapeDtypeStruct((8, 128), jnp.float32)


def behind(array, token):
    return array + token[0, 0].astype(array.dtype)


def in_hbm(*arrays):
    return [pltpu.with_memory_space_constraint(array, pltpu.HBM) for array in arrays]


def own_gradient(rows, own, other, partner, temp, waits):
    height, width = rows.shape
    hbm, vmem = pl.BlockSpec(memory_space=pltpu.HBM), pl.BlockSpec(memory_space=pltpu.VMEM)
    return pl.pallas_call(
        functools.partial(own_body, temp, len(waits)),
        in_specs=[hbm, hbm, hbm, vmem] + [hbm] * len(waits),
        out_specs=[vmem, vmem, vmem],
        out_shape=[
            pltpu.VMEM((height, width), jnp.float32),
            pltpu.VMEM((height, width), rows.dtype),
            TOKEN,
        ],
        scratch_shapes=[
            pltpu.VMEM((2 * height, width), rows.dtype),
            pltpu.VMEM((2, BLOCK, 2 * height), jnp.bfloat16),
            pltpu.SemaphoreType.DMA((3,)),
        ],
        compiler_params=pltpu.CompilerParams(vmem_limit_bytes=20 * 2**20),
        cost_estimate=pl.CostEstimate(
            flops=8 * height * height * width, bytes_accessed=6 * height * width, transcendentals=4 * height * height
        ),
    )(*in_hbm(rows, own, other), partner, *in_hbm(*waits))


def visit_body(sizes, temp, last, waits, *refs):
    count = len(sizes)
    kept, before, others = refs[:2], refs[2:4], refs[4 : 4 + count]
    refs = refs[4 + count + waits :]
    out, (token, stack, weight, sems, *rest) = refs[:2], refs[2:]
    token[...] = jnp.zeros_like(token)
    copies = []
    for side in (0, 1):
        at = 0
        for i, size in enumerate(sizes):
            source = others[i].at[pl.ds(side * size, size)]
            copies.append(pltpu.make_async_copy(source, stack.at[side, pl.ds(at, size)], sems.at[side, i]))
            at += size
    for copy in copies:
        copy.start()
    sent = []
    for side in (0, 1):
        for copy in copies[side * count : (side + 1) * count]:
            copy.wait()
        for b in range(kept[side].shape[0] // BLOCK):
            here = slice(b * BLOCK, (b + 1) * BLOCK)
            grads = gradient(kept[side][here, :], stack.at[side], weight.at[b % 2], temp, None)
            if not last:
                out[side][here, :] = before[side][here, :] + grads
                continue
            result, result_sems = rest
            result[side, here, :] = before[side][here, :] + grads
            rows = pl.ds(b * BLOCK, BLOCK)
            copy = pltpu.make_async_copy(result.at[side, rows], out[side].at[rows], result_sems.at[side, b])
            copy.start()
            sent.append(copy)
    for copy in sent:
        copy.wait()


def visit(kept, before, others, temp, last, waits):
    height, width = kept[0].shape
    sizes = tuple(other.shape[0] // 2 for other in others)
    many, count = sum(sizes), len(sizes)
    hbm, vmem = pl.BlockSpec(memory_space=pltpu.HBM), pl.BlockSpec(memory_space=pltpu.VMEM)
    kept = [pltpu.with_memory_space_constraint(array, pltpu.VMEM) for array in kept]
    before = [pltpu.with_memory_space_constraint(array, pltpu.VMEM) for array in before]
    scratch = [
        pltpu.VMEM((2, many, width), kept[0].dtype),
        pltpu.VMEM((2, BLOCK, many), jnp.bfloat16),
        pltpu.SemaphoreType.DMA((2, count)),
    ]
    if last:
        out_shape = [jax.ShapeDtypeStruct((height, width), jnp.float32)] * 2
        scratch += [pltpu.VMEM((2, height, width), jnp.float32), pltpu.SemaphoreType.DMA((2, height // BLOCK))]
    else:
        out_shape = [pltpu.VMEM((height, width), jnp.float32)] * 2
    return pl.pallas_call(
        functools.partial(visit_body, sizes, temp, last, len(waits)),
        in_specs=[vmem] * 4 + [hbm] * (count + len(waits)),
        out_specs=[hbm if last else vmem] * 2 + [vmem],
        out_shape=out_shape + [TOKEN],
        scratch_shapes=scratch,
        input_output_aliases={} if last else {2: 0, 3: 1},
        compiler_params=pltpu.CompilerParams(vmem_limit_bytes=20 * 2**20),
        cost_estimate=pl.CostEstimate(
            flops=8 * height * many * width, bytes_accessed=4 * many * width, transcendentals=4 * height * many
        ),
    )(*kept, *before, *in_hbm(*others, *waits))


def shards(images, texts, image_partner, text_partner):
    height, width = images.shape
    temp = 2.0 * width ** (-0.5)
    index = lax.axis_index(AXES)
    even = (index & 1) == 0
    first_passes_on = (index & 1) == ((index >> 1) & 1)
    pieces = []
    at = 0
    for size in PIECES:
        pieces.append(jnp.concatenate([texts[at : at + size], images[at : at + size]], axis=0))
        at += size

    partner_texts = lax.ppermute(texts, AXES, CORE_SWAP)
    partner_images = lax.ppermute(images, AXES, CORE_SWAP)
    one = [lax.ppermute(piece, AXES, HALF_SWAP) for piece in pieces[:2]]
    across = lax.ppermute(pieces[1], AXES, ACROSS)

    start = index * height
    total_images, kept_images, token = own_gradient(
        images, texts, partner_texts, (image_partner - start)[:, None], temp, ()
    )
    total_texts, kept_texts, token = own_gradient(
        texts, images, partner_images, (text_partner - start)[:, None], temp, (token,)
    )
    kept, totals = (kept_images, kept_texts), (total_images, total_texts)

    two = [lax.ppermute(one[0], AXES, HAND_ON), lax.ppermute(one[1], AXES, HAND_ON_WITHIN)]
    ahead = [lax.ppermute(piece, AXES, AHEAD) for piece in pieces[2:]]
    back = [lax.ppermute(piece, AXES, BEHIND) for piece in pieces[2:]]

    near = lax.ppermute(behind(jnp.where(first_passes_on, one[0], two[0]), token), AXES, CORE_SWAP)
    *totals, token = visit(kept, totals, [one[0], two[0], near], temp, False, ())
    near = lax.ppermute(behind(jnp.where(even, ahead[0], back[0]), token), AXES, CORE_SWAP)
    two[1] = behind(two[1] + across, token)
    far = lax.ppermute(jnp.where(first_passes_on, one[1], two[1]), AXES, CORE_SWAP)
    *totals, token = visit(kept, totals, [ahead[0], back[0], near, one[1], two[1], far], temp, False, ())
    near = lax.ppermute(behind(jnp.where(even, ahead[1], back[1]), token), AXES, CORE_SWAP)
    *totals, token = visit(kept, totals, [ahead[1], back[1], near], temp, True, ())
    return tuple(totals)


def solution(mesh):
    return jax.shard_map(
        shards,
        mesh=mesh,
        in_specs=(P(AXES, None), P(AXES, None), P(AXES), P(AXES)),
        out_specs=(P(AXES, None), P(AXES, None)),
        check_vma=False,
    )
```

```python
import functools

import jax
import jax.numpy as jnp
from jax import lax
from jax.experimental import pallas as pl
from jax.experimental.pallas import tpu as pltpu
from jax.sharding import PartitionSpec as P

AXES = ("grp", "dev")
LOG2E = 1.4426950408889634
NT = (((1,), (1,)), ((), ()))
BLOCK = 448
STEP = 256
PIECES = (288, 288, 192, 128)
DEVICES = range(128)
NO_COVER = pl.CostEstimate(flops=1, bytes_accessed=1, transcendentals=0)


CORE_SWAP = [(d, d ^ 1) for d in DEVICES]
HALF_SWAP = [(d, d ^ 2) for d in DEVICES]
HAND_ON = [(d, (d + 4 if d & 2 == 0 else d - 4) % 128) for d in DEVICES]
HAND_ON_WITHIN = [(d, to) for d, to in HAND_ON if (d >> 6) == (to >> 6)]
AHEAD = [(d, (d - 2) % 128) for d in DEVICES]
BEHIND = [(d, (d + 2) % 128) for d in DEVICES]


ACROSS = [(62, 64), (63, 65), (64, 62), (65, 63), (126, 0), (127, 1), (0, 126), (1, 127)]


def weights(product, temp, positive):
    exponent = product * (-temp * LOG2E) + 2.0 * LOG2E
    if positive is None:
        return (temp / (1.0 + jnp.exp2(exponent))).astype(jnp.bfloat16)
    exponent = jnp.where(positive, -exponent, exponent)
    return (jnp.where(positive, -temp, temp) / (1.0 + jnp.exp2(exponent))).astype(jnp.bfloat16)


def gradient(left, stack, weight, temp, partner):
    many = stack.shape[0]
    for at in range(0, many, STEP):
        end = min(many, at + STEP)
        product = lax.dot_general(left, stack[at:end, :], NT, preferred_element_type=jnp.float32)
        positive = None
        if partner is not None and at < many // 2:
            positive = partner == at + lax.broadcasted_iota(jnp.int32, product.shape, 1)
        weight[:, at:end] = weights(product, temp, positive)
    return jnp.dot(weight[...], stack[...], preferred_element_type=jnp.float32)


def own_body(temp, waits, rows, own, other, partner, *refs):
    total, kept, token, stack, weight, sems = refs[waits:]
    token[...] = jnp.zeros_like(token)
    height = kept.shape[0]
    copies = [
        pltpu.make_async_copy(rows, kept, sems.at[0]),
        pltpu.make_async_copy(own, stack.at[pl.ds(0, height)], sems.at[1]),
        pltpu.make_async_copy(other, stack.at[pl.ds(height, height)], sems.at[2]),
    ]
    for copy in copies:
        copy.start()
    for copy in copies:
        copy.wait()
    for b in range(height // BLOCK):
        here = slice(b * BLOCK, (b + 1) * BLOCK)
        total[here, :] = gradient(kept[here, :], stack, weight.at[b % 2], temp, partner[here, :])


TOKEN = jax.ShapeDtypeStruct((8, 128), jnp.float32)


def behind(array, token):
    return array + token[0, 0].astype(array.dtype)


def in_hbm(*arrays):
    return [pltpu.with_memory_space_constraint(array, pltpu.HBM) for array in arrays]


def own_gradient(rows, own, other, partner, temp, waits):
    height, width = rows.shape
    hbm, vmem = pl.BlockSpec(memory_space=pltpu.HBM), pl.BlockSpec(memory_space=pltpu.VMEM)
    return pl.pallas_call(
        functools.partial(own_body, temp, len(waits)),
        in_specs=[hbm, hbm, hbm, vmem] + [hbm] * len(waits),
        out_specs=[vmem, vmem, vmem],
        out_shape=[
            pltpu.VMEM((height, width), jnp.float32),
            pltpu.VMEM((height, width), rows.dtype),
            TOKEN,
        ],
        scratch_shapes=[
            pltpu.VMEM((2 * height, width), rows.dtype),
            pltpu.VMEM((2, BLOCK, 2 * height), jnp.bfloat16),
            pltpu.SemaphoreType.DMA((3,)),
        ],
        compiler_params=pltpu.CompilerParams(vmem_limit_bytes=14 * 2**20),
        cost_estimate=pl.CostEstimate(
            flops=8 * height * height * width, bytes_accessed=6 * height * width, transcendentals=4 * height * height
        ),
    )(*in_hbm(rows, own, other), partner, *in_hbm(*waits))


def visit_body(sizes, temp, last, waits, *refs):
    count = len(sizes)
    kept, before, others = refs[:2], refs[2:4], refs[4 : 4 + count]
    refs = refs[4 + count + waits :]
    out, (token, stack, weight, sems, *rest) = refs[:2], refs[2:]
    token[...] = jnp.zeros_like(token)
    copies = []
    for side in (0, 1):
        at = 0
        for i, size in enumerate(sizes):
            source = others[i].at[pl.ds(side * size, size)]
            copies.append(pltpu.make_async_copy(source, stack.at[side, pl.ds(at, size)], sems.at[side, i]))
            at += size
    for copy in copies:
        copy.start()
    sent = []
    for side in (0, 1):
        for copy in copies[side * count : (side + 1) * count]:
            copy.wait()
        for b in range(kept[side].shape[0] // BLOCK):
            here = slice(b * BLOCK, (b + 1) * BLOCK)
            grads = gradient(kept[side][here, :], stack.at[side], weight.at[b % 2], temp, None)
            if not last:
                out[side][here, :] = before[side][here, :] + grads
                continue
            result, result_sems = rest
            result[side, here, :] = before[side][here, :] + grads
            rows = pl.ds(b * BLOCK, BLOCK)
            copy = pltpu.make_async_copy(result.at[side, rows], out[side].at[rows], result_sems.at[side, b])
            copy.start()
            sent.append(copy)
    for copy in sent:
        copy.wait()


def visit(kept, before, others, temp, last, waits):
    height, width = kept[0].shape
    sizes = tuple(other.shape[0] // 2 for other in others)
    many, count = sum(sizes), len(sizes)
    hbm, vmem = pl.BlockSpec(memory_space=pltpu.HBM), pl.BlockSpec(memory_space=pltpu.VMEM)
    kept = [pltpu.with_memory_space_constraint(array, pltpu.VMEM) for array in kept]
    before = [pltpu.with_memory_space_constraint(array, pltpu.VMEM) for array in before]
    scratch = [
        pltpu.VMEM((2, many, width), kept[0].dtype),
        pltpu.VMEM((2, BLOCK, many), jnp.bfloat16),
        pltpu.SemaphoreType.DMA((2, count)),
    ]
    if last:
        out_shape = [jax.ShapeDtypeStruct((height, width), jnp.float32)] * 2
        scratch += [pltpu.VMEM((2, height, width), jnp.float32), pltpu.SemaphoreType.DMA((2, height // BLOCK))]
    else:
        out_shape = [pltpu.VMEM((height, width), jnp.float32)] * 2
    return pl.pallas_call(
        functools.partial(visit_body, sizes, temp, last, len(waits)),
        in_specs=[vmem] * 4 + [hbm] * (count + len(waits)),
        out_specs=[hbm if last else vmem] * 2 + [vmem],
        out_shape=out_shape + [TOKEN],
        scratch_shapes=scratch,
        input_output_aliases={} if last else {2: 0, 3: 1},
        compiler_params=pltpu.CompilerParams(vmem_limit_bytes=14 * 2**20),
        cost_estimate=pl.CostEstimate(
            flops=8 * height * many * width, bytes_accessed=4 * many * width, transcendentals=4 * height * many
        ),
    )(*kept, *before, *in_hbm(*others, *waits))


def shards(images, texts, image_partner, text_partner):
    height, width = images.shape
    temp = 2.0 * width ** (-0.5)
    index = lax.axis_index(AXES)
    even = (index & 1) == 0
    first_passes_on = (index & 1) == ((index >> 1) & 1)
    pieces = []
    at = 0
    for size in PIECES:
        pieces.append(jnp.concatenate([texts[at : at + size], images[at : at + size]], axis=0))
        at += size

    partner_texts = lax.ppermute(texts, AXES, CORE_SWAP)
    partner_images = lax.ppermute(images, AXES, CORE_SWAP)
    one = [lax.ppermute(piece, AXES, HALF_SWAP) for piece in pieces[:2]]
    across = [lax.ppermute(rows, AXES, ACROSS) for rows in (pieces[1][: PIECES[1]], pieces[1][PIECES[1] :])]

    start = index * height
    total_images, kept_images, token = own_gradient(
        images, texts, partner_texts, (image_partner - start)[:, None], temp, (pieces[2], pieces[3])
    )
    total_texts, kept_texts, token = own_gradient(
        texts, images, partner_images, (text_partner - start)[:, None], temp, (token, across[0])
    )
    kept, totals = (kept_images, kept_texts), (total_images, total_texts)

    two = [lax.ppermute(one[0], AXES, HAND_ON), lax.ppermute(one[1], AXES, HAND_ON_WITHIN)]
    ahead = [lax.ppermute(piece, AXES, AHEAD) for piece in pieces[2:]]
    back = [lax.ppermute(piece, AXES, BEHIND) for piece in pieces[2:]]

    near = lax.ppermute(behind(jnp.where(first_passes_on, one[0], two[0]), token), AXES, CORE_SWAP)
    *totals, token = visit(kept, totals, [one[0], two[0], near], temp, False, (across[1],))
    near = lax.ppermute(behind(jnp.where(even, ahead[0], back[0]), token), AXES, CORE_SWAP)
    two[1] = behind(two[1] + jnp.concatenate(across, axis=0), token)
    far = lax.ppermute(jnp.where(first_passes_on, one[1], two[1]), AXES, CORE_SWAP)
    *totals, token = visit(kept, totals, [ahead[0], back[0], near, one[1], two[1], far], temp, False, ())
    near = lax.ppermute(behind(jnp.where(even, ahead[1], back[1]), token), AXES, CORE_SWAP)
    *totals, token = visit(kept, totals, [ahead[1], back[1], near], temp, True, ())
    return tuple(totals)


def solution(mesh):
    return jax.shard_map(
        shards,
        mesh=mesh,
        in_specs=(P(AXES, None), P(AXES, None), P(AXES), P(AXES)),
        out_specs=(P(AXES, None), P(AXES, None)),
        check_vma=False,
    )
```

```python
import functools

import jax
import jax.numpy as jnp
from jax import lax
from jax.experimental import pallas as pl
from jax.experimental.pallas import tpu as pltpu
from jax.sharding import PartitionSpec as P

AXES = ("grp", "dev")
LOG2E = 1.4426950408889634
NT = (((1,), (1,)), ((), ()))
BLOCK = 448
STEP = 256
PIECES = (288, 288, 192, 128)
DEVICES = range(128)
NO_COVER = pl.CostEstimate(flops=1, bytes_accessed=1, transcendentals=0)


CORE_SWAP = [(d, d ^ 1) for d in DEVICES]
HALF_SWAP = [(d, d ^ 2) for d in DEVICES]
HAND_ON = [(d, (d + 4 if d & 2 == 0 else d - 4) % 128) for d in DEVICES]
HAND_ON_WITHIN = [(d, to) for d, to in HAND_ON if (d >> 6) == (to >> 6)]
AHEAD = [(d, (d - 2) % 128) for d in DEVICES]
BEHIND = [(d, (d + 2) % 128) for d in DEVICES]


ACROSS = [(62, 64), (63, 65), (64, 62), (65, 63), (126, 0), (127, 1), (0, 126), (1, 127)]


def weights(product, temp, positive):
    exponent = product * (-temp * LOG2E) + 2.0 * LOG2E
    if positive is None:
        return (temp / (1.0 + jnp.exp2(exponent))).astype(jnp.bfloat16)
    exponent = jnp.where(positive, -exponent, exponent)
    return (jnp.where(positive, -temp, temp) / (1.0 + jnp.exp2(exponent))).astype(jnp.bfloat16)


def gradient(left, stack, weight, temp, partner):
    many = stack.shape[0]
    for at in range(0, many, STEP):
        end = min(many, at + STEP)
        product = lax.dot_general(left, stack[at:end, :], NT, preferred_element_type=jnp.float32)
        positive = None
        if partner is not None and at < many // 2:
            positive = partner == at + lax.broadcasted_iota(jnp.int32, product.shape, 1)
        weight[:, at:end] = weights(product, temp, positive)
    return jnp.dot(weight[...], stack[...], preferred_element_type=jnp.float32)


def own_body(temp, waits, rows, own, other, partner, *refs):
    total, kept, token, stack, weight, sems = refs[waits:]
    token[...] = jnp.zeros_like(token)
    height = kept.shape[0]
    copies = [
        pltpu.make_async_copy(rows, kept, sems.at[0]),
        pltpu.make_async_copy(own, stack.at[pl.ds(0, height)], sems.at[1]),
        pltpu.make_async_copy(other, stack.at[pl.ds(height, height)], sems.at[2]),
    ]
    for copy in copies:
        copy.start()
    for copy in copies:
        copy.wait()
    for b in range(height // BLOCK):
        here = slice(b * BLOCK, (b + 1) * BLOCK)
        total[here, :] = gradient(kept[here, :], stack, weight.at[b % 2], temp, partner[here, :])


TOKEN = jax.ShapeDtypeStruct((8, 128), jnp.float32)


def behind(array, token):
    return array + token[0, 0].astype(array.dtype)


def in_hbm(*arrays):
    return [pltpu.with_memory_space_constraint(array, pltpu.HBM) for array in arrays]


def own_gradient(rows, own, other, partner, temp, waits):
    height, width = rows.shape
    hbm, vmem = pl.BlockSpec(memory_space=pltpu.HBM), pl.BlockSpec(memory_space=pltpu.VMEM)
    return pl.pallas_call(
        functools.partial(own_body, temp, len(waits)),
        in_specs=[hbm, hbm, hbm, vmem] + [hbm] * len(waits),
        out_specs=[vmem, vmem, vmem],
        out_shape=[
            pltpu.VMEM((height, width), jnp.float32),
            pltpu.VMEM((height, width), rows.dtype),
            TOKEN,
        ],
        scratch_shapes=[
            pltpu.VMEM((2 * height, width), rows.dtype),
            pltpu.VMEM((2, BLOCK, 2 * height), jnp.bfloat16),
            pltpu.SemaphoreType.DMA((3,)),
        ],
        compiler_params=pltpu.CompilerParams(vmem_limit_bytes=14 * 2**20),
        cost_estimate=pl.CostEstimate(
            flops=8 * height * height * width, bytes_accessed=6 * height * width, transcendentals=4 * height * height
        ),
    )(*in_hbm(rows, own, other), partner, *in_hbm(*waits))


def visit_body(sizes, temp, last, waits, split, *refs):
    count = len(sizes) + split
    kept, before, others = refs[:2], refs[2:4], refs[4 : 4 + count]
    refs = refs[4 + count + waits :]
    out, (token, stack, weight, sems, *rest) = refs[:2], refs[2:]
    token[...] = jnp.zeros_like(token)
    copies = []
    for side in (0, 1):
        at = 0
        for i, size in enumerate(sizes):
            ref = others[i + side] if split and i == count - 2 else others[i]
            source = ref if split and i == count - 2 else ref.at[pl.ds(side * size, size)]
            copies.append(pltpu.make_async_copy(source, stack.at[side, pl.ds(at, size)], sems.at[side, i]))
            at += size
    for copy in copies:
        copy.start()
    sent = []
    for side in (0, 1):
        for copy in copies[side * len(sizes) : (side + 1) * len(sizes)]:
            copy.wait()
        for b in range(kept[side].shape[0] // BLOCK):
            here = slice(b * BLOCK, (b + 1) * BLOCK)
            grads = gradient(kept[side][here, :], stack.at[side], weight.at[b % 2], temp, None)
            if not last:
                out[side][here, :] = before[side][here, :] + grads
                continue
            result, result_sems = rest
            result[side, here, :] = before[side][here, :] + grads
            rows = pl.ds(b * BLOCK, BLOCK)
            copy = pltpu.make_async_copy(result.at[side, rows], out[side].at[rows], result_sems.at[side, b])
            copy.start()
            sent.append(copy)
    for copy in sent:
        copy.wait()


def visit(kept, before, others, temp, last, waits, split=False):
    height, width = kept[0].shape
    sizes = tuple(other.shape[0] // 2 for other in others)
    if split:
        sizes = sizes[:-2] + (others[-1].shape[0],)
    many, count = sum(sizes), len(others)
    hbm, vmem = pl.BlockSpec(memory_space=pltpu.HBM), pl.BlockSpec(memory_space=pltpu.VMEM)
    kept = [pltpu.with_memory_space_constraint(array, pltpu.VMEM) for array in kept]
    before = [pltpu.with_memory_space_constraint(array, pltpu.VMEM) for array in before]
    scratch = [
        pltpu.VMEM((2, many, width), kept[0].dtype),
        pltpu.VMEM((2, BLOCK, many), jnp.bfloat16),
        pltpu.SemaphoreType.DMA((2, count)),
    ]
    if last:
        out_shape = [jax.ShapeDtypeStruct((height, width), jnp.float32)] * 2
        scratch += [pltpu.VMEM((2, height, width), jnp.float32), pltpu.SemaphoreType.DMA((2, height // BLOCK))]
    else:
        out_shape = [pltpu.VMEM((height, width), jnp.float32)] * 2
    return pl.pallas_call(
        functools.partial(visit_body, sizes, temp, last, len(waits), split),
        in_specs=[vmem] * 4 + [hbm] * (count + len(waits)),
        out_specs=[hbm if last else vmem] * 2 + [vmem],
        out_shape=out_shape + [TOKEN],
        scratch_shapes=scratch,
        input_output_aliases={} if last else {2: 0, 3: 1},
        compiler_params=pltpu.CompilerParams(vmem_limit_bytes=14 * 2**20),
        cost_estimate=pl.CostEstimate(
            flops=8 * height * many * width, bytes_accessed=4 * many * width, transcendentals=4 * height * many
        ),
    )(*kept, *before, *in_hbm(*others, *waits))


def shards(images, texts, image_partner, text_partner):
    height, width = images.shape
    temp = 2.0 * width ** (-0.5)
    index = lax.axis_index(AXES)
    even = (index & 1) == 0
    first_passes_on = (index & 1) == ((index >> 1) & 1)
    pieces = []
    at = 0
    for size in PIECES:
        pieces.append(jnp.concatenate([texts[at : at + size], images[at : at + size]], axis=0))
        at += size

    partner_texts = lax.ppermute(texts, AXES, CORE_SWAP)
    partner_images = lax.ppermute(images, AXES, CORE_SWAP)
    one = [lax.ppermute(piece, AXES, HALF_SWAP) for piece in pieces[:2]]
    across = [lax.ppermute(rows, AXES, ACROSS) for rows in (pieces[1][: PIECES[1]], pieces[1][PIECES[1] :])]

    start = index * height
    total_images, kept_images, token = own_gradient(
        images, texts, partner_texts, (image_partner - start)[:, None], temp, (pieces[2], pieces[3])
    )
    total_texts, kept_texts, token = own_gradient(
        texts, images, partner_images, (text_partner - start)[:, None], temp, (token, across[0])
    )
    kept, totals = (kept_images, kept_texts), (total_images, total_texts)

    two = [lax.ppermute(one[0], AXES, HAND_ON), lax.ppermute(one[1], AXES, HAND_ON_WITHIN)]
    ahead = [lax.ppermute(piece, AXES, AHEAD) for piece in pieces[2:]]
    back = [lax.ppermute(piece, AXES, BEHIND) for piece in pieces[2:]]

    near = lax.ppermute(behind(jnp.where(first_passes_on, one[0], two[0]), token), AXES, CORE_SWAP)
    *totals, token = visit(kept, totals, [one[0], two[0], near], temp, False, (across[1],))
    near = lax.ppermute(behind(jnp.where(even, ahead[0], back[0]), token), AXES, CORE_SWAP)
    handed = two[1] + jnp.concatenate(across, axis=0)
    far = lax.ppermute(behind(jnp.where(first_passes_on, one[1], handed), token), AXES, CORE_SWAP)
    others = [ahead[0], back[0], near, one[1], two[1], far, *across]
    *totals, token = visit(kept, totals, others, temp, False, (), split=True)
    near = lax.ppermute(behind(jnp.where(even, ahead[1], back[1]), token), AXES, CORE_SWAP)
    *totals, token = visit(kept, totals, [ahead[1], back[1], near], temp, True, ())
    return tuple(totals)


def solution(mesh):
    return jax.shard_map(
        shards,
        mesh=mesh,
        in_specs=(P(AXES, None), P(AXES, None), P(AXES), P(AXES)),
        out_specs=(P(AXES, None), P(AXES, None)),
        check_vma=False,
    )
```
